256 devices in a mesh: dev: 256 (over z, y, x, core).
Axes of the slice: x: 4, y: 4, z: 8, core: 2. Of those that a mesh axis runs over, the one named last changes fastest.
Arguments:
- descriptors: bfloat16 [262144, 2048], P('dev'), may hold values from -0.5 to 1.5
- probes: bfloat16 [262144, 256], P('dev'), may hold values from -6 to 6
- plan: int32 [2, 256], replicated, may hold values from 0 to 255, as said below
Outputs:
- kernel_probes: float32 [262144, 256], P('dev')
- rayleigh: float32 [256], replicated
The draws below stay inside these ranges and needn't reach their ends.
Inputs may be any that keep to these rules, and one draw needn't show every extreme that they name: In each round r there is one power of two m_r below 256 with plan[r, a] = a XOR m_r for every block a; the m_r of different rounds differ.
All inputs are finite; a program needn't handle non-finite values.
Results may differ from the reference program's by a relative error of at most 0.00075.
Values may be sent and summed in bfloat16 or wider, within the bound.
No kernel may reach another device: no remote copies, remote signals or barrier semaphores. Data moves between devices by JAX's collectives and lax.ppermute only.
A program may use at most 64 MiB of HBM per device.

```python
import jax
import jax.numpy as jnp
from jax import lax

D = 2048
PROBES = 256
ROWS_DEV = 1024
ROUNDS = 2
ROWS = 262144
DEVICES = 256


def draw_plan(key, part):
    key = jax.random.fold_in(key, 7)
    levels = DEVICES.bit_length() - 1
    first_key = jax.random.fold_in(key, 11)
    second_key = jax.random.fold_in(key, 23)
    first = jax.random.randint(first_key, (), 0, levels, dtype=jnp.int32)
    offset = jax.random.randint(second_key, (), 1, levels, dtype=jnp.int32)
    second = jnp.remainder(first + offset, levels).astype(jnp.int32)
    chosen = jnp.stack([first, second]).astype(jnp.int32)[:ROUNDS]
    masks = jnp.left_shift(jnp.int32(1), chosen).astype(jnp.int32)
    blocks = jnp.arange(DEVICES, dtype=jnp.int32)
    return jnp.bitwise_xor(blocks[None, :], masks[:, None]).astype(jnp.int32)


def level_of(key, extent, cuts, least, high):
    def one(position, shards_of):
        heights = jax.random.uniform(jax.random.fold_in(jax.random.fold_in(key, 6), position), (shards_of,), jnp.float32, least / len(cuts), high / len(cuts))
        return jnp.repeat(jnp.exp(heights), extent[position] // shards_of).reshape((-1,) + (1,) * (len(extent) - position - 1))

    factor_of = one(*cuts[0])
    for cut in cuts[1:]:
        factor_of = factor_of * one(*cut)
    return factor_of


def bell_draw(own_key, dims, spread, limit, split=(), kind=jnp.bfloat16):
    drawn = spread * jax.random.normal(own_key, dims, jnp.float32)
    if split:
        drawn = drawn * level_of(own_key, dims, split, -0.22, 0.18)
    return jnp.clip(drawn, -limit, limit).astype(kind)


def setup_inputs(seed: int = 0) -> dict:
    arg_keys = jax.random.split(jax.random.key(seed), 4)
    descriptors = jnp.clip(-0.5 + 2.0 * jax.random.uniform(arg_keys[0], (ROWS, D), jnp.float32) ** level_of(arg_keys[0], (ROWS, D), ((0, 256),), -0.2, 0.2), -0.5, 1.5).astype(jnp.bfloat16)
    probes = bell_draw(arg_keys[1], (ROWS, PROBES), 1.0, 6.0, ((0, 256),))
    plan = draw_plan(jax.random.fold_in(arg_keys[3], 71), 0)
    return {"descriptors": descriptors, "probes": probes, "plan": plan}


def make_tile(left, left_norms, right, right_norms):
    dots = lax.dot_general(left, right, (((1,), (1,)), ((), ())), preferred_element_type=jnp.float32)
    cosine = dots / (left_norms[:, None] * right_norms[None, :])
    return (cosine ** 4).astype(jnp.bfloat16)

def reference(descriptors, probes, plan):
    wide = descriptors.astype(jnp.float32)
    norms = jnp.sqrt(lax.optimization_barrier(jnp.sum(wide * wide, axis=1)))
    blocks = descriptors.reshape(DEVICES, ROWS_DEV, D)
    norm_blocks = norms.reshape(DEVICES, ROWS_DEV)
    probe_blocks = probes.reshape(DEVICES, ROWS_DEV, PROBES)

    def one_block(index):
        own = blocks[index]
        own_norms = norm_blocks[index]
        tile = make_tile(own, own_norms, own, own_norms)
        total = jnp.dot(tile, probe_blocks[index], preferred_element_type=jnp.float32)
        for step in range(ROUNDS):
            other = plan[step, index]
            tile = make_tile(own, own_norms, blocks[other], norm_blocks[other])
            total = total + jnp.dot(tile, probe_blocks[other], preferred_element_type=jnp.float32)
        return total
    kernel_probes = lax.map(one_block, jnp.arange(DEVICES, dtype=jnp.int32)).reshape(ROWS, PROBES)
    values = probes.astype(jnp.float32)
    rayleigh = lax.optimization_barrier(jnp.sum(values * kernel_probes, axis=0)) / lax.optimization_barrier(jnp.sum(values * values, axis=0))
    return (kernel_probes, rayleigh)
```

```python
from functools import partial

import jax
import jax.numpy as jnp
from jax import lax
from jax.experimental import pallas as pl
from jax.experimental.pallas import tpu as pltpu
from jax.sharding import PartitionSpec as P

LEVELS = 8
DEVICES = 1 << LEVELS
CHUNKS = (192, 448, 256, 128)
COLS = 256
AXIS_OF = (0, 1, 1, 2, 2, 3, 3, 3)
RELAYED = ((1, 2), (3, 4), (5, 7), (6, 7))

NT = (((1,), (1,)), ((), ()))
NN = (((1,), (0,)), ((), ()))
TN = (((0,), (0,)), ((), ()))
VMEM = pl.BlockSpec(memory_space=pltpu.VMEM)
SMEM = pl.BlockSpec(memory_space=pltpu.SMEM)


def dot(left, right, dims):
    return lax.dot_general(left, right, dims, preferred_element_type=jnp.float32)


def inverse_norms(block):
    wide = block.astype(jnp.float32)
    return 1.0 / jnp.sqrt(jnp.sum(wide * wide, axis=1, keepdims=True))


def make_tile(left, left_inverse, right, right_inverse):
    cosine = dot(left, right, NT) * left_inverse * right_inverse
    square = cosine * cosine
    return (square * square).astype(jnp.bfloat16)


def row_block(step):
    return pl.ds(pl.multiple_of(step * COLS, COLS), COLS)


def own_kernel(own, own_probes, total, sums, inverse, column):
    def norms(step, _):
        rows = row_block(step)
        wide = jnp.broadcast_to(inverse_norms(own[rows, :]), (COLS, 128))
        column[rows, :] = wide
        inverse[step] = jnp.transpose(wide)[0:1, :]
        return 0

    def tiles(step, _):
        rows = row_block(step)
        tile = make_tile(own[...], column[:, 0:1], own[rows, :], inverse[step])
        total[...] += dot(tile, own_probes[rows, :], NN)
        return 0

    steps = own.shape[0] // COLS
    lax.fori_loop(0, steps, norms, 0)
    total[...] = jnp.zeros_like(total)
    lax.fori_loop(0, steps, tiles, 0)
    values = own_probes[...].astype(jnp.float32)
    sums[0:1, :] = jnp.sum(values * total[...], axis=0, keepdims=True)
    sums[1:2, :] = jnp.sum(values * values, axis=0, keepdims=True)


def own_block(own, own_probes):
    rows, depth = own.shape
    count = own_probes.shape[1]
    return pl.pallas_call(
        own_kernel,
        out_shape=(
            jax.ShapeDtypeStruct((rows, count), jnp.float32),
            jax.ShapeDtypeStruct((2, count), jnp.float32),
            jax.ShapeDtypeStruct((rows // COLS, 1, COLS), jnp.float32),
        ),
        in_specs=[VMEM] * 2,
        out_specs=[VMEM] * 3,
        scratch_shapes=[pltpu.VMEM((rows, 128), jnp.float32)],
        compiler_params=pltpu.CompilerParams(vmem_limit_bytes=32 * 2**20),
        cost_estimate=pl.CostEstimate(
            flops=2 * rows * rows * (depth + count), bytes_accessed=rows * (depth + 2 * count) * 2, transcendentals=0
        ),
        name="own_block",
    )(own, own_probes)


def pair_kernel(own, own_probes, inverse, sums_in, other, total_in, *rest):
    valid, (back, total, sums) = rest[:-3], rest[-3:]
    depth = own.shape[1]

    def work():
        block, block_probes = other.at[:, :depth], other.at[:, depth:]
        back[...] = jnp.zeros_like(back)
        left_inverse = inverse_norms(block[...])

        def tiles(step, _):
            rows = row_block(step)
            tile = make_tile(block[...], left_inverse, own[rows, :], inverse[step])
            back[...] += dot(tile, own_probes[rows, :], NN)
            total[rows, :] = total_in[rows, :] + dot(tile, block_probes[...], TN)
            return 0

        lax.fori_loop(0, own.shape[0] // COLS, tiles, 0)
        share = jnp.sum(block_probes[...].astype(jnp.float32) * back[...], axis=0, keepdims=True)
        sums[0:1, :] = sums_in[0:1, :] + (share + share)
        sums[1:2, :] = sums_in[1:2, :]

    if not valid:
        work()
        return
    pl.when(valid[0][0] != 0)(work)

    @pl.when(valid[0][0] == 0)
    def _():
        total[...] = total_in[...]
        sums[...] = sums_in[...]


def pair_block(own, own_probes, inverse, sums, other, total, valid=None):
    rows, depth = other.shape[0], own.shape[1]
    count = own_probes.shape[1]
    flags = [] if valid is None else [valid]
    return pl.pallas_call(
        pair_kernel,
        out_shape=(
            jax.ShapeDtypeStruct((rows, count), jnp.float32),
            jax.ShapeDtypeStruct(total.shape, jnp.float32),
            jax.ShapeDtypeStruct(sums.shape, jnp.float32),
        ),
        in_specs=[VMEM] * 6 + [SMEM] * len(flags),
        out_specs=[VMEM] * 3,
        input_output_aliases={5: 1},
        compiler_params=pltpu.CompilerParams(vmem_limit_bytes=32 * 2**20),
        cost_estimate=pl.CostEstimate(
            flops=2 * rows * own.shape[0] * (depth + 2 * count),
            bytes_accessed=(rows + own.shape[0]) * depth * 2,
            transcendentals=0,
        ),
        name="pair_block",
    )(own, own_probes, inverse, sums, other, total, *flags)


def send(block, route):
    return lax.ppermute(block, "dev", route)


def reverse(route):
    return [(b, a) for a, b in route]


def first_kind(device, low, high):
    turn = device & 1 if low > 0 else 0
    return (device >> low & 1) ^ (device >> high & 1) ^ turn == 0


def groups_over(bits):
    spread = [sum((i >> n & 1) << bit for n, bit in enumerate(bits)) for i in range(1 << len(bits))]
    return [[base | s for s in spread] for base in range(DEVICES) if base & spread[-1] == 0]


def sum_over_bits(sums, bits):
    copies = jnp.broadcast_to(sums[None], (1 << len(bits), *sums.shape))
    return jnp.sum(lax.all_to_all(copies, "dev", 0, 0, axis_index_groups=groups_over(bits)), axis=0)


def sum_over_devices(sums, low, high):
    busy = {AXIS_OF[low], AXIS_OF[high]}
    free = [bit for bit in range(LEVELS) if AXIS_OF[bit] not in busy][-5:]
    rest = [bit for bit in range(LEVELS) if bit not in free]
    return sum_over_bits(sum_over_bits(sums, free), rest)


def pieces_of(own, own_probes):
    starts = [sum(CHUNKS[:i]) for i in range(len(CHUNKS))]
    cuts = [slice(s, s + n) for s, n in zip(starts, CHUNKS)]
    return [jnp.concatenate([own[cut], own_probes[cut]], axis=1) for cut in cuts]


def ring_of_four(low, high, own, own_probes):
    route = [(i, i ^ 1 << (low if first_kind(i, low, high) else high)) for i in range(DEVICES)]
    others = [send(piece, route) for piece in pieces_of(own, own_probes)]
    total, sums, inverse = own_block(own, own_probes)
    backs = []
    for other in others:
        back, total, sums = pair_block(own, own_probes, inverse, sums, other, total)
        backs.append(back)
    returned = send(jnp.concatenate(backs), reverse(route))
    sums = sum_over_devices(sums, low, high)
    return total + returned, sums[0] / sums[1]


def relayed(low, high, own, own_probes):
    near = [(i, i ^ 1 << low) for i in range(DEVICES) if first_kind(i, low, high)]
    passed = [(i, i ^ 1 << low ^ 1 << high) for _, i in near]
    far = [(i, i ^ 1 << high) for i, _ in near]
    me = lax.axis_index("dev")
    mine = (me >> low ^ me >> high ^ (me if low > 0 else 0)) & 1
    valid = mine.astype(jnp.int32).reshape(1)
    firsts = [send(piece, near) for piece in pieces_of(own, own_probes)]
    total, sums, inverse = own_block(own, own_probes)
    firsts = [lax.optimization_barrier((first, inverse))[0] for first in firsts]
    seconds = [send(first, passed) for first in firsts]
    backs = [[], []]
    for pair in zip(firsts, seconds):
        for which, other in enumerate(pair):
            back, total, sums = pair_block(own, own_probes, inverse, sums, other, total, valid)
            backs[which].append(back)
    backs = [jnp.concatenate(back) for back in backs]
    for route, back in zip((near, far), backs):
        total = total + send(back, reverse(route))
    sums = sum_over_devices(sums, low, high)
    return total, sums[0] / sums[1]


def one_plan(low, high, own, own_probes):
    way = relayed if (low, high) in RELAYED else ring_of_four
    return way(low, high, own, own_probes)


PAIRS = [(low, high) for high in range(LEVELS) for low in range(high)]


def local(descriptors, probes, plan):
    masks = plan[:, 0]
    both = masks[0] + masks[1]
    powers = [1 << bit for bit in range(LEVELS)]
    high = sum((both >= power).astype(jnp.int32) for power in powers[1:])
    rest = both - (jnp.int32(1) << high)
    low = sum((rest >= power).astype(jnp.int32) for power in powers[1:])
    which = high * (high - 1) // 2 + low
    return lax.switch(which, [partial(one_plan, *pair) for pair in PAIRS], descriptors, probes)


def solution(mesh):
    in_specs = (P("dev", None), P("dev", None), P())
    out_specs = (P("dev", None), P())
    return jax.shard_map(local, mesh=mesh, in_specs=in_specs, out_specs=out_specs, check_vma=False)
```

```python
from functools import partial

import jax
import jax.numpy as jnp
from jax import lax
from jax.experimental import pallas as pl
from jax.experimental.pallas import tpu as pltpu
from jax.sharding import PartitionSpec as P

LEVELS = 8
DEVICES = 1 << LEVELS
COLS = 256
XY, CORE_Z = (1, 2, 3, 4), (0, 5, 6, 7)

NT = (((1,), (1,)), ((), ()))
NN = (((1,), (0,)), ((), ()))
TN = (((0,), (0,)), ((), ()))
VMEM = pl.BlockSpec(memory_space=pltpu.VMEM)
SMEM = pl.BlockSpec(memory_space=pltpu.SMEM)
ANY = pl.BlockSpec(memory_space=pl.ANY)
LIMIT = pltpu.CompilerParams(vmem_limit_bytes=40 * 2**20)


def dot(left, right, dims):
    return lax.dot_general(left, right, dims, preferred_element_type=jnp.float32)


def floats(*shape):
    return jax.ShapeDtypeStruct(shape, jnp.float32)


def inverse_norms(block):
    wide = block.astype(jnp.float32)
    return 1.0 / jnp.sqrt(jnp.sum(wide * wide, axis=1, keepdims=True))


def make_tile(left, left_inverse, right, right_inverse):
    cosine = dot(left, right, NT) * left_inverse * right_inverse
    square = cosine * cosine
    return (square * square).astype(jnp.bfloat16)


def work_kernel(odd, own, own_probes, low, low_probes, high, high_probes, back, total, sums,
                here, here_probes, there, there_probes, column, done, probes_done):
    parts = own.shape[0] // COLS
    cuts = [pl.ds(part * COLS, COLS) for part in range(parts)]

    def own_copy(part):
        return pltpu.make_async_copy(own.at[cuts[part]], here.at[cuts[part]], done.at[part])

    def other_copies(block, probes):
        return (
            pltpu.make_async_copy(probes, there_probes, probes_done.at[1]),
            pltpu.make_async_copy(block, there, done.at[parts]),
        )

    def row_of(inverse):
        return jnp.transpose(jnp.broadcast_to(inverse, (COLS, 128)))[0:1, :]

    mine = pltpu.make_async_copy(own_probes, here_probes, probes_done.at[0])
    own_copy(parts - 1).start()
    mine.start()
    for part in reversed(range(parts - 1)):
        own_copy(part).start()

    @pl.when(odd[0] != 0)
    def _():
        for copy in other_copies(low, low_probes):
            copy.start()

    @pl.when(odd[0] == 0)
    def _():
        for copy in other_copies(high, high_probes):
            copy.start()

    rows = [None] * parts
    mine.wait()
    for part in reversed(range(parts)):
        own_copy(part).wait()
        inverse = inverse_norms(here[cuts[part], :])
        column[cuts[part], :] = jnp.broadcast_to(inverse, (COLS, 128))
        rows[part] = row_of(inverse)
        under = pl.ds(part * COLS, (parts - part) * COLS)
        tile = make_tile(here[under, :], column[under, 0:1], here[cuts[part], :], rows[part])
        product = dot(tile, here_probes[cuts[part], :], NN)
        if part == parts - 1:
            total[cuts[part], :] = product
        else:
            rest = pl.ds((part + 1) * COLS, (parts - part - 1) * COLS)
            total[rest, :] += product[COLS:]
            total[cuts[part], :] = product[:COLS] + dot(tile[COLS:], here_probes[rest, :], TN)
    values = here_probes[...].astype(jnp.float32)
    share = jnp.sum(values * total[...], axis=0, keepdims=True)
    sums[1:2, :] = jnp.sum(values * values, axis=0, keepdims=True)
    for copy in other_copies(low, low_probes):
        copy.wait()
    column[...] = jnp.broadcast_to(inverse_norms(there[...]), column.shape)
    for part in range(parts):
        tile = make_tile(there[...], column[:, 0:1], here[cuts[part], :], rows[part])
        product = dot(tile, here_probes[cuts[part], :], NN)
        if part == 0:
            back[...] = product
        else:
            back[...] += product
        total[cuts[part], :] += dot(tile, there_probes[...], TN)
    pair_share = jnp.sum(there_probes[...].astype(jnp.float32) * back[...], axis=0, keepdims=True)
    sums[0:1, :] = share + (pair_share + pair_share)


def work(odd, own, own_probes, low, low_probes, high, high_probes):
    n, depth = own.shape
    count = own_probes.shape[1]
    parts = n // COLS
    return pl.pallas_call(
        work_kernel,
        out_shape=(floats(n, count), floats(n, count), floats(2, count)),
        in_specs=[SMEM] + [ANY] * 6,
        out_specs=[VMEM] * 3,
        scratch_shapes=[
            pltpu.VMEM((n, depth), jnp.bfloat16),
            pltpu.VMEM((n, count), jnp.bfloat16),
            pltpu.VMEM((n, depth), jnp.bfloat16),
            pltpu.VMEM((n, count), jnp.bfloat16),
            pltpu.VMEM((n, 128), jnp.float32),
            pltpu.SemaphoreType.DMA((parts + 1,)),
            pltpu.SemaphoreType.DMA((2,)),
        ],
        compiler_params=LIMIT,
        cost_estimate=pl.CostEstimate(
            flops=2 * n * n * (2 * depth + 3 * count), bytes_accessed=2 * n * depth * 2, transcendentals=0
        ),
        name="own_and_pair",
    )(odd, own, own_probes, low, low_probes, high, high_probes)


def parity(device):
    for shift in (4, 2, 1):
        device = device ^ device >> shift
    return device & 1


def route(bit, odd):
    return [(i, i ^ 1 << bit) for i in range(DEVICES) if parity(i) == odd]


def send(block, bit, odd):
    return lax.ppermute(block, "dev", route(bit, odd))


def groups_over(bits):
    spread = [sum((i >> n & 1) << bit for n, bit in enumerate(bits)) for i in range(1 << len(bits))]
    return [[base | s for s in spread] for base in range(DEVICES) if base & spread[-1] == 0]


def sum_over_bits(sums, bits):
    copies = jnp.broadcast_to(sums[None], (1 << len(bits), *sums.shape))
    return jnp.sum(lax.all_to_all(copies, "dev", 0, 0, axis_index_groups=groups_over(bits)), axis=0)


def exchange(low, high, own, own_probes):
    return [send(x, bit, odd) for bit, odd in ((low, 0), (high, 1)) for x in (own_probes, own)]


def give_back(low, high, back):
    return send(back, low, 1) + send(back, high, 0)


PAIRS = [(low, high) for high in range(LEVELS) for low in range(high)]


def local(descriptors, probes, plan):
    masks = plan[:, 0]
    both = masks[0] + masks[1]
    powers = [1 << bit for bit in range(LEVELS)]
    high = sum((both >= power).astype(jnp.int32) for power in powers[1:])
    rest = both - (jnp.int32(1) << high)
    low = sum((rest >= power).astype(jnp.int32) for power in powers[1:])
    which = high * (high - 1) // 2 + low
    odd = parity(lax.axis_index("dev")).astype(jnp.int32).reshape(1)
    low_probes, low_block, high_probes, high_block = lax.switch(
        which, [partial(exchange, *pair) for pair in PAIRS], descriptors, probes
    )
    back, total, sums = work(odd, descriptors, probes, low_block, low_probes, high_block, high_probes)
    returned = lax.switch(which, [partial(give_back, *pair) for pair in PAIRS], back)
    sums = sum_over_bits(sum_over_bits(sums, XY), CORE_Z)
    return total + returned, sums[0] / sums[1]


def solution(mesh):
    in_specs = (P("dev", None), P("dev", None), P())
    out_specs = (P("dev", None), P())
    return jax.shard_map(local, mesh=mesh, in_specs=in_specs, out_specs=out_specs, check_vma=False)
```

```python
from functools import partial

import jax
import jax.numpy as jnp
from jax import lax
from jax.experimental import pallas as pl
from jax.experimental.pallas import tpu as pltpu
from jax.sharding import PartitionSpec as P

LEVELS = 8
DEVICES = 1 << LEVELS
COLS = 256
XY, CORE_Z = (1, 2, 3, 4), (0, 5, 6, 7)

NT = (((1,), (1,)), ((), ()))
NN = (((1,), (0,)), ((), ()))
TN = (((0,), (0,)), ((), ()))
VMEM = pl.BlockSpec(memory_space=pltpu.VMEM)
SMEM = pl.BlockSpec(memory_space=pltpu.SMEM)
ANY = pl.BlockSpec(memory_space=pl.ANY)
LIMIT = pltpu.CompilerParams(vmem_limit_bytes=40 * 2**20)


def dot(left, right, dims):
    return lax.dot_general(left, right, dims, preferred_element_type=jnp.float32)


def floats(*shape):
    return jax.ShapeDtypeStruct(shape, jnp.float32)


def inverse_norms(block):
    wide = block.astype(jnp.float32)
    return 1.0 / jnp.sqrt(jnp.sum(wide * wide, axis=1, keepdims=True))


def make_tile(left, left_inverse, right, right_inverse):
    cosine = dot(left, right, NT) * left_inverse * right_inverse
    square = cosine * cosine
    return (square * square).astype(jnp.bfloat16)


def row_block(step):
    return pl.ds(pl.multiple_of(step * COLS, COLS), COLS)


def work_kernel(odd, own, own_probes, low, low_probes, high, high_probes, back, total, sums,
                here, here_probes, there, there_probes, column, inverse, done):
    steps = own.shape[0] // COLS
    mine = (pltpu.make_async_copy(own, here, done.at[0]), pltpu.make_async_copy(own_probes, here_probes, done.at[1]))
    for copy in mine:
        copy.start()

    def other_copies(block, probes):
        return pltpu.make_async_copy(block, there, done.at[2]), pltpu.make_async_copy(probes, there_probes, done.at[3])

    @pl.when(odd[0] != 0)
    def _():
        for copy in other_copies(low, low_probes):
            copy.start()

    @pl.when(odd[0] == 0)
    def _():
        for copy in other_copies(high, high_probes):
            copy.start()

    for copy in mine:
        copy.wait()

    def norms(step, _):
        rows = row_block(step)
        wide = jnp.broadcast_to(inverse_norms(here[rows, :]), (COLS, 128))
        column[rows, :] = wide
        inverse[step] = jnp.transpose(wide)[0:1, :]
        return 0

    def own_tiles(step, _):
        rows = row_block(step)
        tile = make_tile(here[...], column[:, 0:1], here[rows, :], inverse[step])
        total[...] += dot(tile, here_probes[rows, :], NN)
        return 0

    def other_norms(step, _):
        rows = row_block(step)
        column[rows, :] = jnp.broadcast_to(inverse_norms(there[rows, :]), (COLS, 128))
        return 0

    def pair_tiles(step, _):
        rows = row_block(step)
        tile = make_tile(there[...], column[:, 0:1], here[rows, :], inverse[step])
        back[...] += dot(tile, here_probes[rows, :], NN)
        total[rows, :] += dot(tile, there_probes[...], TN)
        return 0

    def shares(step, _):
        rows = row_block(step)
        values, others = here_probes[rows, :].astype(jnp.float32), there_probes[rows, :].astype(jnp.float32)
        pair = jnp.sum(others * back[rows, :], axis=0, keepdims=True)
        sums[0:1, :] += pair + pair
        sums[1:2, :] += jnp.sum(values * values, axis=0, keepdims=True)
        return 0

    def own_shares(step, _):
        rows = row_block(step)
        sums[0:1, :] += jnp.sum(here_probes[rows, :].astype(jnp.float32) * total[rows, :], axis=0, keepdims=True)
        return 0

    total[...] = jnp.zeros_like(total)
    back[...] = jnp.zeros_like(back)
    sums[...] = jnp.zeros_like(sums)
    lax.fori_loop(0, steps, norms, 0)
    lax.fori_loop(0, steps, own_tiles, 0)
    lax.fori_loop(0, steps, own_shares, 0)
    for copy in other_copies(low, low_probes):
        copy.wait()
    lax.fori_loop(0, steps, other_norms, 0)
    lax.fori_loop(0, steps, pair_tiles, 0)
    lax.fori_loop(0, steps, shares, 0)


def work(odd, own, own_probes, low, low_probes, high, high_probes):
    n, depth = own.shape
    count = own_probes.shape[1]
    return pl.pallas_call(
        work_kernel,
        out_shape=(floats(n, count), floats(n, count), floats(2, count)),
        in_specs=[SMEM] + [ANY] * 6,
        out_specs=[VMEM] * 3,
        scratch_shapes=[
            pltpu.VMEM((n, depth), jnp.bfloat16),
            pltpu.VMEM((n, count), jnp.bfloat16),
            pltpu.VMEM((n, depth), jnp.bfloat16),
            pltpu.VMEM((n, count), jnp.bfloat16),
            pltpu.VMEM((n, 128), jnp.float32),
            pltpu.VMEM((n // COLS, 1, COLS), jnp.float32),
            pltpu.SemaphoreType.DMA((4,)),
        ],
        compiler_params=LIMIT,
        cost_estimate=pl.CostEstimate(
            flops=2 * n * n * (2 * depth + 3 * count), bytes_accessed=2 * n * depth * 2, transcendentals=0
        ),
        name="own_and_pair",
    )(odd, own, own_probes, low, low_probes, high, high_probes)


def parity(device):
    for shift in (4, 2, 1):
        device = device ^ device >> shift
    return device & 1


def route(bit, odd):
    return [(i, i ^ 1 << bit) for i in range(DEVICES) if parity(i) == odd]


def send(block, bit, odd):
    return lax.ppermute(block, "dev", route(bit, odd))


def groups_over(bits):
    spread = [sum((i >> n & 1) << bit for n, bit in enumerate(bits)) for i in range(1 << len(bits))]
    return [[base | s for s in spread] for base in range(DEVICES) if base & spread[-1] == 0]


def sum_over_bits(sums, bits):
    copies = jnp.broadcast_to(sums[None], (1 << len(bits), *sums.shape))
    return jnp.sum(lax.all_to_all(copies, "dev", 0, 0, axis_index_groups=groups_over(bits)), axis=0)


def exchange(low, high, own, own_probes):
    return [send(x, bit, odd) for bit, odd in ((low, 0), (high, 1)) for x in (own_probes, own)]


def give_back(low, high, back):
    return send(back, low, 1) + send(back, high, 0)


PAIRS = [(low, high) for high in range(LEVELS) for low in range(high)]


def local(descriptors, probes, plan):
    masks = plan[:, 0]
    both = masks[0] + masks[1]
    powers = [1 << bit for bit in range(LEVELS)]
    high = sum((both >= power).astype(jnp.int32) for power in powers[1:])
    rest = both - (jnp.int32(1) << high)
    low = sum((rest >= power).astype(jnp.int32) for power in powers[1:])
    which = high * (high - 1) // 2 + low
    odd = parity(lax.axis_index("dev")).astype(jnp.int32).reshape(1)
    low_probes, low_block, high_probes, high_block = lax.switch(
        which, [partial(exchange, *pair) for pair in PAIRS], descriptors, probes
    )
    back, total, sums = work(odd, descriptors, probes, low_block, low_probes, high_block, high_probes)
    returned = lax.switch(which, [partial(give_back, *pair) for pair in PAIRS], back)
    sums = sum_over_bits(sum_over_bits(sums, XY), CORE_Z)
    return total + returned, sums[0] / sums[1]


def solution(mesh):
    in_specs = (P("dev", None), P("dev", None), P())
    out_specs = (P("dev", None), P())
    return jax.shard_map(local, mesh=mesh, in_specs=in_specs, out_specs=out_specs, check_vma=False)
```

```python
from functools import partial

import jax
import jax.numpy as jnp
from jax import lax
from jax.experimental import pallas as pl
from jax.experimental.pallas import tpu as pltpu
from jax.sharding import PartitionSpec as P

LEVELS = 8
DEVICES = 1 << LEVELS
COLS = 256
EXTRA = 16
XY, CORE_Z = (1, 2, 3, 4), (0, 5, 6, 7)

NT = (((1,), (1,)), ((), ()))
NN = (((1,), (0,)), ((), ()))
TN = (((0,), (0,)), ((), ()))
VMEM = pl.BlockSpec(memory_space=pltpu.VMEM)
SMEM = pl.BlockSpec(memory_space=pltpu.SMEM)
ANY = pl.BlockSpec(memory_space=pl.ANY)
LIMIT = pltpu.CompilerParams(vmem_limit_bytes=40 * 2**20)


def dot(left, right, dims):
    return lax.dot_general(left, right, dims, preferred_element_type=jnp.float32)


def floats(*shape):
    return jax.ShapeDtypeStruct(shape, jnp.float32)


def inverse_norms(block):
    wide = block.astype(jnp.float32)
    return 1.0 / jnp.sqrt(jnp.sum(wide * wide, axis=1, keepdims=True))


def make_tile(left, left_inverse, right, right_inverse):
    cosine = dot(left, right, NT) * left_inverse * right_inverse
    square = cosine * cosine
    return (square * square).astype(jnp.bfloat16)


def row_block(step):
    return pl.ds(pl.multiple_of(step * COLS, COLS), COLS)


def work_kernel(odd, own, own_probes, low, low_probes, high, high_probes, sent, total, sums,
                here, here_probes, there, there_probes, column, inverse, back, done):
    steps = own.shape[0] // COLS
    mine = (pltpu.make_async_copy(own, here, done.at[0]), pltpu.make_async_copy(own_probes, here_probes, done.at[1]))
    for copy in mine:
        copy.start()

    def other_copies(block, probes):
        return pltpu.make_async_copy(block, there, done.at[2]), pltpu.make_async_copy(probes, there_probes, done.at[3])

    @pl.when(odd[0] != 0)
    def _():
        for copy in other_copies(low, low_probes):
            copy.start()

    @pl.when(odd[0] == 0)
    def _():
        for copy in other_copies(high, high_probes):
            copy.start()

    for copy in mine:
        copy.wait()

    def norms(step, _):
        rows = row_block(step)
        wide = jnp.broadcast_to(inverse_norms(here[rows, :]), (COLS, 128))
        column[rows, :] = wide
        inverse[step] = jnp.transpose(wide)[0:1, :]
        return 0

    def own_tiles(step, _):
        rows = row_block(step)
        tile = make_tile(here[...], column[:, 0:1], here[rows, :], inverse[step])
        total[...] += dot(tile, here_probes[rows, :], NN)
        return 0

    def other_norms(step, _):
        rows = row_block(step)
        column[rows, :] = jnp.broadcast_to(inverse_norms(there[rows, :]), (COLS, 128))
        return 0

    def pair_tiles(step, _):
        rows = row_block(step)
        tile = make_tile(there[...], column[:, 0:1], here[rows, :], inverse[step])
        back[...] += dot(tile, here_probes[rows, :], NN)
        total[rows, :] += dot(tile, there_probes[...], TN)
        return 0

    def shares(step, _):
        rows = row_block(step)
        values, others = here_probes[rows, :].astype(jnp.float32), there_probes[rows, :].astype(jnp.float32)
        pair = jnp.sum(others * back[rows, :], axis=0, keepdims=True)
        sums[0:1, :] += pair + pair
        sums[1:2, :] += jnp.sum(values * values, axis=0, keepdims=True)
        return 0

    def own_shares(step, _):
        rows = row_block(step)
        sums[0:1, :] += jnp.sum(here_probes[rows, :].astype(jnp.float32) * total[rows, :], axis=0, keepdims=True)
        return 0

    total[...] = jnp.zeros_like(total)
    back[...] = jnp.zeros_like(back)
    sums[...] = jnp.zeros_like(sums)
    lax.fori_loop(0, steps, norms, 0)
    lax.fori_loop(0, steps, own_tiles, 0)
    lax.fori_loop(0, steps, own_shares, 0)
    for copy in other_copies(low, low_probes):
        copy.wait()
    lax.fori_loop(0, steps, other_norms, 0)
    lax.fori_loop(0, steps, pair_tiles, 0)
    lax.fori_loop(0, steps, shares, 0)
    peak = jnp.max(jnp.abs(back[...]), axis=0, keepdims=True)
    power = jnp.clip(jnp.ceil(jnp.log2(peak)), -100.0, 20.0)
    scale = jnp.exp2(-power)

    def scaled(step, _):
        rows = row_block(step)
        sent[rows, :] = back[rows, :] * scale
        return 0

    lax.fori_loop(0, steps, scaled, 0)
    sent[steps * COLS :, :] = jnp.broadcast_to(power, (EXTRA, power.shape[1]))


def work(odd, own, own_probes, low, low_probes, high, high_probes):
    n, depth = own.shape
    count = own_probes.shape[1]
    return pl.pallas_call(
        work_kernel,
        out_shape=(floats(n + EXTRA, count), floats(n, count), floats(2, count)),
        in_specs=[SMEM] + [ANY] * 6,
        out_specs=[VMEM] * 3,
        scratch_shapes=[
            pltpu.VMEM((n, depth), jnp.bfloat16),
            pltpu.VMEM((n, count), jnp.bfloat16),
            pltpu.VMEM((n, depth), jnp.bfloat16),
            pltpu.VMEM((n, count), jnp.bfloat16),
            pltpu.VMEM((n, 128), jnp.float32),
            pltpu.VMEM((n // COLS, 1, COLS), jnp.float32),
            pltpu.VMEM((n, count), jnp.float32),
            pltpu.SemaphoreType.DMA((4,)),
        ],
        compiler_params=LIMIT,
        cost_estimate=pl.CostEstimate(
            flops=2 * n * n * (2 * depth + 3 * count), bytes_accessed=2 * n * depth * 2, transcendentals=0
        ),
        name="own_and_pair",
    )(odd, own, own_probes, low, low_probes, high, high_probes)


def parity(device):
    for shift in (4, 2, 1):
        device = device ^ device >> shift
    return device & 1


def route(bit, odd):
    return [(i, i ^ 1 << bit) for i in range(DEVICES) if parity(i) == odd]


def send(block, bit, odd):
    return lax.ppermute(block, "dev", route(bit, odd))


def groups_over(bits):
    spread = [sum((i >> n & 1) << bit for n, bit in enumerate(bits)) for i in range(1 << len(bits))]
    return [[base | s for s in spread] for base in range(DEVICES) if base & spread[-1] == 0]


def sum_over_bits(sums, bits):
    copies = jnp.broadcast_to(sums[None], (1 << len(bits), *sums.shape))
    return jnp.sum(lax.all_to_all(copies, "dev", 0, 0, axis_index_groups=groups_over(bits)), axis=0)


def exchange(low, high, own, own_probes):
    return [send(x, bit, odd) for bit, odd in ((low, 0), (high, 1)) for x in (own_probes, own)]


def give_back(low, high, back):
    return send(back, low, 1) + send(back, high, 0)


PAIRS = [(low, high) for high in range(LEVELS) for low in range(high)]


def local(descriptors, probes, plan):
    masks = plan[:, 0]
    both = masks[0] + masks[1]
    powers = [1 << bit for bit in range(LEVELS)]
    high = sum((both >= power).astype(jnp.int32) for power in powers[1:])
    rest = both - (jnp.int32(1) << high)
    low = sum((rest >= power).astype(jnp.int32) for power in powers[1:])
    which = high * (high - 1) // 2 + low
    odd = parity(lax.axis_index("dev")).astype(jnp.int32).reshape(1)
    low_probes, low_block, high_probes, high_block = lax.switch(
        which, [partial(exchange, *pair) for pair in PAIRS], descriptors, probes
    )
    sent, total, sums = work(odd, descriptors, probes, low_block, low_probes, high_block, high_probes)
    sent = sent.astype(jnp.float16)
    returned = lax.switch(which, [partial(give_back, *pair) for pair in PAIRS], sent).astype(jnp.float32)
    returned = returned[:-EXTRA] * jnp.exp2(returned[-EXTRA])
    sums = sum_over_bits(sum_over_bits(sums, XY), CORE_Z)
    return total + returned, sums[0] / sums[1]


def solution(mesh):
    in_specs = (P("dev", None), P("dev", None), P())
    out_specs = (P("dev", None), P())
    return jax.shard_map(local, mesh=mesh, in_specs=in_specs, out_specs=out_specs, check_vma=False)
```

```python
from functools import partial

import jax
import jax.numpy as jnp
from jax import lax
from jax.experimental import pallas as pl
from jax.experimental.pallas import tpu as pltpu
from jax.sharding import PartitionSpec as P

LEVELS = 8
DEVICES = 1 << LEVELS
COLS = 256
EXTRA = 16
XY, CORE_Z = (1, 2, 3, 4), (0, 5, 6, 7)

NT = (((1,), (1,)), ((), ()))
NN = (((1,), (0,)), ((), ()))
TN = (((0,), (0,)), ((), ()))
VMEM = pl.BlockSpec(memory_space=pltpu.VMEM)
SMEM = pl.BlockSpec(memory_space=pltpu.SMEM)
ANY = pl.BlockSpec(memory_space=pl.ANY)
LIMIT = pltpu.CompilerParams(vmem_limit_bytes=40 * 2**20)


def dot(left, right, dims):
    return lax.dot_general(left, right, dims, preferred_element_type=jnp.float32)


def floats(*shape):
    return jax.ShapeDtypeStruct(shape, jnp.float32)


def inverse_norms(block):
    wide = block.astype(jnp.float32)
    return 1.0 / jnp.sqrt(jnp.sum(wide * wide, axis=1, keepdims=True))


def make_tile(left, left_inverse, right, right_inverse):
    cosine = dot(left, right, NT) * left_inverse * right_inverse
    square = cosine * cosine
    return (square * square).astype(jnp.bfloat16)


def row_block(step):
    return pl.ds(pl.multiple_of(step * COLS, COLS), COLS)


def work_kernel(odd, own, own_probes, low, low_probes, high, high_probes, sent, total, sums,
                here, here_probes, there, there_probes, column, inverse, back, done):
    steps = own.shape[0] // COLS
    mine = (pltpu.make_async_copy(own, here, done.at[0]), pltpu.make_async_copy(own_probes, here_probes, done.at[1]))
    for copy in mine:
        copy.start()

    def other_copies(block, probes):
        return pltpu.make_async_copy(block, there, done.at[2]), pltpu.make_async_copy(probes, there_probes, done.at[3])

    @pl.when(odd[0] != 0)
    def _():
        for copy in other_copies(low, low_probes):
            copy.start()

    @pl.when(odd[0] == 0)
    def _():
        for copy in other_copies(high, high_probes):
            copy.start()

    for copy in mine:
        copy.wait()

    def norms(step, _):
        rows = row_block(step)
        wide = jnp.broadcast_to(inverse_norms(here[rows, :]), (COLS, 128))
        column[rows, :] = wide
        inverse[step] = jnp.transpose(wide)[0:1, :]
        return 0

    def own_tiles(step, _):
        rows = row_block(step)
        tile = make_tile(here[...], column[:, 0:1], here[rows, :], inverse[step])
        total[...] += dot(tile, here_probes[rows, :], NN)
        return 0

    def other_norms(step, _):
        rows = row_block(step)
        column[rows, :] = jnp.broadcast_to(inverse_norms(there[rows, :]), (COLS, 128))
        return 0

    def pair_tiles(step, _):
        rows = row_block(step)
        tile = make_tile(there[...], column[:, 0:1], here[rows, :], inverse[step])
        back[...] += dot(tile, here_probes[rows, :], NN)
        total[rows, :] += dot(tile, there_probes[...], TN)
        return 0

    def shares(step, _):
        rows = row_block(step)
        values, others = here_probes[rows, :].astype(jnp.float32), there_probes[rows, :].astype(jnp.float32)
        pair = jnp.sum(others * back[rows, :], axis=0, keepdims=True)
        sums[0:1, :] += pair + pair
        sums[1:2, :] += jnp.sum(values * values, axis=0, keepdims=True)
        return 0

    def own_shares(step, _):
        rows = row_block(step)
        sums[0:1, :] += jnp.sum(here_probes[rows, :].astype(jnp.float32) * total[rows, :], axis=0, keepdims=True)
        return 0

    total[...] = jnp.zeros_like(total)
    back[...] = jnp.zeros_like(back)
    sums[...] = jnp.zeros_like(sums)
    lax.fori_loop(0, steps, norms, 0)
    lax.fori_loop(0, steps, own_tiles, 0)
    lax.fori_loop(0, steps, own_shares, 0)
    for copy in other_copies(low, low_probes):
        copy.wait()
    lax.fori_loop(0, steps, other_norms, 0)
    lax.fori_loop(0, steps, pair_tiles, 0)
    lax.fori_loop(0, steps, shares, 0)
    peak = jnp.max(jnp.abs(back[...]), axis=0, keepdims=True)
    power = jnp.clip(jnp.ceil(jnp.log2(peak)), -100.0, 20.0)
    scale = jnp.exp2(-power)

    def scaled(step, _):
        rows = row_block(step)
        sent[rows, :] = back[rows, :] * scale
        return 0

    lax.fori_loop(0, steps, scaled, 0)
    sent[steps * COLS :, :] = jnp.broadcast_to(power, (EXTRA, power.shape[1]))


def work(odd, own, own_probes, low, low_probes, high, high_probes):
    n, depth = own.shape
    count = own_probes.shape[1]
    return pl.pallas_call(
        work_kernel,
        out_shape=(floats(n + EXTRA, count), floats(n, count), floats(2, count)),
        in_specs=[SMEM] + [ANY] * 6,
        out_specs=[VMEM] * 3,
        scratch_shapes=[
            pltpu.VMEM((n, depth), jnp.bfloat16),
            pltpu.VMEM((n, count), jnp.bfloat16),
            pltpu.VMEM((n, depth), jnp.bfloat16),
            pltpu.VMEM((n, count), jnp.bfloat16),
            pltpu.VMEM((n, 128), jnp.float32),
            pltpu.VMEM((n // COLS, 1, COLS), jnp.float32),
            pltpu.VMEM((n, count), jnp.float32),
            pltpu.SemaphoreType.DMA((4,)),
        ],
        compiler_params=LIMIT,
        cost_estimate=pl.CostEstimate(
            flops=2 * n * n * (2 * depth + 3 * count), bytes_accessed=2 * n * depth * 2, transcendentals=0
        ),
        name="own_and_pair",
    )(odd, own, own_probes, low, low_probes, high, high_probes)


def parity(device):
    for shift in (4, 2, 1):
        device = device ^ device >> shift
    return device & 1


def route(bit, odd):
    return [(i, i ^ 1 << bit) for i in range(DEVICES) if parity(i) == odd]


def send(block, bit, odd):
    return lax.ppermute(block, "dev", route(bit, odd))


def groups_over(bits):
    spread = [sum((i >> n & 1) << bit for n, bit in enumerate(bits)) for i in range(1 << len(bits))]
    return [[base | s for s in spread] for base in range(DEVICES) if base & spread[-1] == 0]


def sum_over_bits(sums, bits):
    copies = jnp.broadcast_to(sums[None], (1 << len(bits), *sums.shape))
    return jnp.sum(lax.all_to_all(copies, "dev", 0, 0, axis_index_groups=groups_over(bits)), axis=0)


def exchange(low, high, own, own_probes):
    return [send(x, bit, odd) for bit, odd in ((low, 0), (high, 1)) for x in (own_probes, own)]


def give_back(low, high, back):
    return send(back, low, 1), send(back, high, 0)


PAIRS = [(low, high) for high in range(LEVELS) for low in range(high)]


def local(descriptors, probes, plan):
    masks = plan[:, 0]
    both = masks[0] + masks[1]
    powers = [1 << bit for bit in range(LEVELS)]
    high = sum((both >= power).astype(jnp.int32) for power in powers[1:])
    rest = both - (jnp.int32(1) << high)
    low = sum((rest >= power).astype(jnp.int32) for power in powers[1:])
    which = high * (high - 1) // 2 + low
    odd = parity(lax.axis_index("dev")).astype(jnp.int32).reshape(1)
    low_probes, low_block, high_probes, high_block = lax.switch(
        which, [partial(exchange, *pair) for pair in PAIRS], descriptors, probes
    )
    sent, total, sums = work(odd, descriptors, probes, low_block, low_probes, high_block, high_probes)
    sent = sent.astype(jnp.float16)
    pair = lax.switch(which, [partial(give_back, *pair) for pair in PAIRS], sent)
    power = sum(x[-EXTRA].astype(jnp.float32) for x in pair)
    returned = sum(x[:-EXTRA].astype(jnp.float32) for x in pair) * jnp.exp2(power)
    sums = sum_over_bits(sum_over_bits(sums, XY), CORE_Z)
    return total + returned, sums[0] / sums[1]


def solution(mesh):
    in_specs = (P("dev", None), P("dev", None), P())
    out_specs = (P("dev", None), P())
    return jax.shard_map(local, mesh=mesh, in_specs=in_specs, out_specs=out_specs, check_vma=False)
```
